32 devices in a mesh: row: 4 (over z), col: 4 (over x, core), fr: 2 (over y).
Axes of the slice: x: 2, y: 2, z: 4, core: 2. Of those that a mesh axis runs over, the one named last changes fastest.
Arguments:
- sigma_aa: float32 [3072, 12288], P(('fr', 'row'), 'col'), parts along dimension 0, may hold values from -6 to 6
- l_as: float32 [24576, 6144], P(('fr', 'row'), 'col'), parts along dimension 0, may hold values from -0.078125 to 0.078125
- block_mask: int32 [8, 4], P(('fr', 'row'), 'col'), parts along dimension 0, may hold values 0 or 1
Outputs:
- sigma_as: float32 [3072, 6144], P(('fr', 'row'), 'col'), parts along dimension 0
The draws below stay inside these ranges and needn't reach their ends.
There are 2 independent parts, one for each index of `fr`. The reference program is written for one: setup_inputs(seed, part) draws one part's arguments, and reference() takes and returns one part's arrays. A program takes and returns all parts, laid end to end along the dimension named above; each array names one. Nothing has to cross between parts.
All inputs are finite; a program needn't handle non-finite values. No bound on the sum of `block_mask` on one device may be relied on, other than what follows from the above.
Results may differ from the reference program's by a relative error of at most 0.0003.
Values sent between devices are 32-bit elements; how exact they have to be, the bound alone decides.
No kernel may reach another device: no remote copies, remote signals or barrier semaphores. Data moves between devices by JAX's collectives and lax.ppermute only.
A program may use at most 128 MiB of HBM per device.

```python
import jax
import jax.numpy as jnp
from jax import lax

ANC = 12288
SEP = 6144
ROW_DEV = 384
NB = 4
STEPS = 2
ROWS = 1536


def set_ends(array, stream_key, least, largest):
    longest = array.shape.index(max(array.shape))
    spots = []
    for shift in (0, 1):
        where = [jax.random.randint(jax.random.fold_in(stream_key, axis), (), 0, length) for axis, length in enumerate(array.shape)]
        where[longest] = (where[longest] + shift) % array.shape[longest]
        spots.append(tuple(where))
    return array.at[spots[0]].set(least).at[spots[1]].set(largest)


def shard_levels(stream_key, shape, split, smallest, top_value):
    level, own = 1.0, jax.random.fold_in(stream_key, 6)
    for position, shards_of in split:
        draws = jnp.exp(jax.random.uniform(jax.random.fold_in(own, position), (shards_of,), jnp.float32, smallest / len(split), top_value / len(split)))
        level = level * jnp.repeat(draws, shape[position] // shards_of).reshape([-1 if axis == position else 1 for axis in range(len(shape))])
    return level


def normal_values(rng, shape, scale, reach, shards=(), kind=jnp.bfloat16):
    entries = scale * jax.random.normal(rng, shape, jnp.float32)
    if shards:
        entries = entries * shard_levels(rng, shape, shards, -0.22, 0.18)
    return jnp.clip(entries, -reach, reach).astype(kind)


def setup_inputs(seed: int = 0, part: int = 0) -> dict:
    keys = jax.random.split(jax.random.key(seed), 4)
    part_keys = jax.random.split(jax.random.fold_in(keys[3], part), 4)
    sigma_aa = normal_values(part_keys[0], (ROWS, ANC), 1.0, 6.0, ((0, 4), (1, 4)), jnp.float32)
    l_as = normal_values(part_keys[1], (ANC, SEP), (ANC // 2) ** -0.5, 0.078125, ((0, 4), (1, 4)), jnp.float32)
    block_mask = set_ends((jax.random.randint(part_keys[2], (NB, NB), 0, 4) < 3).astype(jnp.int32), jax.random.fold_in(part_keys[2], 1), 0, 1)
    return {"sigma_aa": sigma_aa, "l_as": l_as, "block_mask": block_mask}


def reference(sigma_aa, l_as, block_mask):
    anc_block = ANC // NB
    sep_block = SEP // NB
    mask_full = jnp.repeat(jnp.repeat(block_mask.astype(l_as.dtype), anc_block, 0), sep_block, 1)
    factor = l_as * mask_full
    sigma_blocks = sigma_aa.reshape(NB, ROW_DEV, NB, anc_block)
    factor_blocks = factor.reshape(NB, anc_block, NB, sep_block)
    blocks = jnp.arange(NB, dtype=jnp.int32)

    def one_row(block_row):
        row_panel = sigma_blocks[block_row]
        summed = jnp.zeros((ROW_DEV, NB, sep_block), sigma_aa.dtype)
        for turn in range(STEPS):
            stored_cols = (blocks + turn) % NB
            lhs_block = row_panel[:, stored_cols, :]
            stored_row = (block_row + turn) % NB
            rhs_block = factor_blocks[stored_row]
            summed = summed + jnp.einsum("rja,ajs->rjs", lhs_block, rhs_block, precision=lax.Precision.HIGHEST)
        return -summed

    result = lax.map(one_row, blocks)
    return result.reshape(ROWS, SEP)
```

```python
import jax
import jax.numpy as jnp
from jax import lax
from jax.sharding import PartitionSpec as P


def shifted(block, rows_by, cols_by):
    rows, cols = lax.axis_size("row"), lax.axis_size("col")
    route = [
        (r * cols + c, (r + rows_by) % rows * cols + (c + cols_by) % cols) for r in range(rows) for c in range(cols)
    ]
    return lax.ppermute(block, ("row", "col"), route)


def product(lhs_block, rhs_block):
    return jnp.dot(lhs_block, rhs_block, preferred_element_type=jnp.float32, precision=lax.Precision.HIGH)


def body(sigma_aa, l_as, block_mask):
    half_steps = lax.axis_size("row") // 2
    sign = -block_mask[0, 0].astype(jnp.float32)
    chunks = 2
    size = sigma_aa.shape[0] // chunks
    outs = []
    for chunk in range(chunks):
        own = sigma_aa[chunk * size : (chunk + 1) * size]
        total = None
        for turn in reversed(range(half_steps)):
            visiting = shifted(own, turn, -turn) if turn else own
            term = sign * product(visiting, l_as)
            total = term if total is None else shifted(total, -1, 0) + term
        outs.append(total)
    return jnp.concatenate(outs, 0)


def solution(mesh):
    placed = (P(("fr", "row"), "col"), P(("fr", "row"), "col"), P(("fr", "row"), "col"))
    return jax.shard_map(
        body, mesh=mesh, in_specs=placed, out_specs=P(("fr", "row"), "col"), check_vma=False
    )
```

```python
import jax
import jax.numpy as jnp
from jax import lax
from jax.sharding import PartitionSpec as P


CUTS = (0, 4, 24, 40, 48)
HOLD = {0: 2, 1: 3, 2: 3}


def shifted(block, rows_by, cols_by):
    rows, cols = lax.axis_size("row"), lax.axis_size("col")
    route = [
        (r * cols + c, (r + rows_by) % rows * cols + (c + cols_by) % cols) for r in range(rows) for c in range(cols)
    ]
    return lax.ppermute(block, ("row", "col"), route)


def product(lhs_block, rhs_block):
    return jnp.dot(lhs_block, rhs_block, preferred_element_type=jnp.float32, precision=lax.Precision.HIGH)


def body(sigma_aa, l_as, block_mask):
    half_steps = lax.axis_size("row") // 2
    rows = sigma_aa.shape[0]
    sign = -block_mask[0, 0].astype(jnp.float32)
    cuts = [rows * cut // CUTS[-1] for cut in CUTS]
    pieces = [sigma_aa[a:b] for a, b in zip(cuts, cuts[1:])]
    visits = [[shifted(piece, turn, -turn) for turn in range(1, half_steps)] for piece in pieces]
    own = sign * product(sigma_aa, l_as)
    own, visits[0] = lax.optimization_barrier((own, visits[0]))
    outs = []
    for index, visit in enumerate(visits):
        total = sign * product(visit[-1], l_as)
        later = HOLD.get(index)
        if index + 1 < len(visits):
            anchor, visits[index + 1][-1] = lax.optimization_barrier((total, visits[index + 1][-1]))
        if later is not None:
            total, visits[later][-1] = lax.optimization_barrier((total, visits[later][-1]))
        for visiting in reversed(visit[:-1]):
            total = shifted(total, -1, 0) + sign * product(visiting, l_as)
        outs.append(shifted(total, -1, 0))
    early = jnp.concatenate([*outs[:-1], jnp.zeros_like(outs[-1])], 0) + own
    return lax.dynamic_update_slice(early, outs[-1] + own[cuts[-2] :], (cuts[-2], 0))


def solution(mesh):
    placed = (P(("fr", "row"), "col"), P(("fr", "row"), "col"), P(("fr", "row"), "col"))
    return jax.shard_map(
        body, mesh=mesh, in_specs=placed, out_specs=P(("fr", "row"), "col"), check_vma=False
    )
```

```python
import jax
import jax.numpy as jnp
from jax import lax
from jax.sharding import PartitionSpec as P


CUTS = (0, 4, 26, 46, 48)


def shifted(block, rows_by, cols_by):
    rows, cols = lax.axis_size("row"), lax.axis_size("col")
    route = [
        (r * cols + c, (r + rows_by) % rows * cols + (c + cols_by) % cols) for r in range(rows) for c in range(cols)
    ]
    return lax.ppermute(block, ("row", "col"), route)


def after(value, *others):
    return lax.optimization_barrier((value, *others))[0]


def product(lhs_block, rhs_block):
    return jnp.dot(lhs_block, rhs_block, preferred_element_type=jnp.float32, precision=lax.Precision.HIGH)


def body(sigma_aa, l_as, block_mask):
    half_steps = lax.axis_size("row") // 2
    rows = sigma_aa.shape[0]
    sign = -block_mask[0, 0].astype(jnp.float32)
    cuts = [rows * cut // CUTS[-1] for cut in CUTS]
    pieces, block = [], sigma_aa
    for start, end in zip(cuts, cuts[1:]):
        piece, block = lax.optimization_barrier((block[start:end], block))
        pieces.append(piece)
    visits = [[shifted(piece, turn, -turn) for turn in range(1, half_steps)] for piece in pieces]
    first, second, third, last = [visit[-1] for visit in visits]

    def times_factor(block):
        return sign * product(block, l_as)

    def travel_back(total, piece):
        for visiting in reversed(visits[piece][:-1]):
            total = shifted(total, -1, 0) + times_factor(visiting)
        return shifted(total, -1, 0)

    own = times_factor(sigma_aa)
    first_total = times_factor(after(first, own))
    second_total = times_factor(after(second, first_total))
    first_out = travel_back(after(first_total, second_total, third), 0)
    second_out = travel_back(after(second_total, last), 1)
    third_total = times_factor(after(third, last, first_out))
    third_out = travel_back(third_total, 2)
    last_out = travel_back(times_factor(after(last, third_total)), 3)

    early = jnp.concatenate([first_out, second_out, third_out, jnp.zeros_like(last_out)], 0) + own
    return lax.dynamic_update_slice(early, last_out + own[cuts[3] :], (cuts[3], 0))


def solution(mesh):
    placed = (P(("fr", "row"), "col"), P(("fr", "row"), "col"), P(("fr", "row"), "col"))
    return jax.shard_map(
        body, mesh=mesh, in_specs=placed, out_specs=P(("fr", "row"), "col"), check_vma=False
    )
```

```python
import jax
import jax.numpy as jnp
from jax import lax
from jax.sharding import PartitionSpec as P


CUTS = (0, 4, 26, 46, 48)


def shifted(block, rows_by, cols_by):
    rows, cols = lax.axis_size("row"), lax.axis_size("col")
    route = [
        (r * cols + c, (r + rows_by) % rows * cols + (c + cols_by) % cols) for r in range(rows) for c in range(cols)
    ]
    return lax.ppermute(block, ("row", "col"), route)


def after(value, *others):
    return lax.optimization_barrier((value, *others))[0]


def product(lhs_block, rhs_block):
    return jnp.dot(lhs_block, rhs_block, preferred_element_type=jnp.float32, precision=lax.Precision.HIGH)


def body(sigma_aa, l_as, block_mask):
    half_steps = lax.axis_size("row") // 2
    rows = sigma_aa.shape[0]
    sign = -block_mask[0, 0].astype(jnp.float32)
    cuts = [rows * cut // CUTS[-1] for cut in CUTS]
    pieces, block = [], sigma_aa
    for start, end in zip(cuts, cuts[1:]):
        piece, block = lax.optimization_barrier((block[start:end], block))
        pieces.append(piece)
    visits = [[shifted(piece, turn, -turn) for turn in range(1, half_steps)] for piece in pieces]
    first, second, third, last = [visit[-1] for visit in visits]

    def times_factor(block):
        return sign * product(block, l_as)

    def travel_back(total, piece):
        for visiting in reversed(visits[piece][:-1]):
            total = shifted(total, -1, 0) + times_factor(visiting)
        return shifted(total, -1, 0)

    first_total = times_factor(first)
    own = times_factor(after(sigma_aa, first_total))
    second_total = times_factor(after(second, own))
    first_out = travel_back(after(first_total, second_total, third), 0)
    second_out = travel_back(after(second_total, last), 1)
    third_total = times_factor(after(third, last, first_out))
    third_out = travel_back(third_total, 2)
    last_out = travel_back(times_factor(after(last, third_total)), 3)

    early = jnp.concatenate([first_out, second_out, third_out, jnp.zeros_like(last_out)], 0) + own
    return lax.dynamic_update_slice(early, last_out + own[cuts[3] :], (cuts[3], 0))


def solution(mesh):
    placed = (P(("fr", "row"), "col"), P(("fr", "row"), "col"), P(("fr", "row"), "col"))
    return jax.shard_map(
        body, mesh=mesh, in_specs=placed, out_specs=P(("fr", "row"), "col"), check_vma=False
    )
```

```python
import jax
import jax.numpy as jnp
from jax import lax
from jax.sharding import PartitionSpec as P


CUTS = (0, 4, 27, 46, 48)


def shifted(block, rows_by, cols_by):
    rows, cols = lax.axis_size("row"), lax.axis_size("col")
    route = [
        (r * cols + c, (r + rows_by) % rows * cols + (c + cols_by) % cols) for r in range(rows) for c in range(cols)
    ]
    return lax.ppermute(block, ("row", "col"), route)


def after(value, *others):
    return lax.optimization_barrier((value, *others))[0]


def product(lhs_block, rhs_block):
    return jnp.dot(lhs_block, rhs_block, preferred_element_type=jnp.float32, precision=lax.Precision.HIGH)


def body(sigma_aa, l_as, block_mask):
    half_steps = lax.axis_size("row") // 2
    rows = sigma_aa.shape[0]
    sign = -block_mask[0, 0].astype(jnp.float32)
    cuts = [rows * cut // CUTS[-1] for cut in CUTS]
    pieces, block = [], sigma_aa
    for start, end in zip(cuts, cuts[1:]):
        piece, block = lax.optimization_barrier((block[start:end], block))
        pieces.append(piece)
    visits = [[shifted(piece, turn, -turn) for turn in range(1, half_steps)] for piece in pieces]
    first, second, third, last = [visit[-1] for visit in visits]

    def times_factor(block):
        return sign * product(block, l_as)

    def travel_back(total, piece):
        for visiting in reversed(visits[piece][:-1]):
            total = shifted(total, -1, 0) + times_factor(visiting)
        return shifted(total, -1, 0)

    first_total = times_factor(first)
    own = times_factor(after(sigma_aa, first_total))
    second_total = times_factor(after(second, own))
    first_out = travel_back(after(first_total, second_total, third), 0)
    second_out = travel_back(after(second_total, third), 1)
    third_total = times_factor(after(third, last, first_out))
    third_out = travel_back(third_total, 2)
    last_out = travel_back(times_factor(after(last, third_total)), 3)

    early = jnp.concatenate([first_out, second_out, third_out, jnp.zeros_like(last_out)], 0) + own
    return lax.dynamic_update_slice(early, last_out + own[cuts[3] :], (cuts[3], 0))


def solution(mesh):
    placed = (P(("fr", "row"), "col"), P(("fr", "row"), "col"), P(("fr", "row"), "col"))
    return jax.shard_map(
        body, mesh=mesh, in_specs=placed, out_specs=P(("fr", "row"), "col"), check_vma=False
    )
```

```python
import jax
import jax.numpy as jnp
from jax import lax
from jax.sharding import PartitionSpec as P


CUTS = (0, 4, 28, 46, 48)


def shifted(block, rows_by, cols_by):
    rows, cols = lax.axis_size("row"), lax.axis_size("col")
    route = [
        (r * cols + c, (r + rows_by) % rows * cols + (c + cols_by) % cols) for r in range(rows) for c in range(cols)
    ]
    return lax.ppermute(block, ("row", "col"), route)


def after(value, *others):
    return lax.optimization_barrier((value, *others))[0]


def product(lhs_block, rhs_block):
    return jnp.dot(lhs_block, rhs_block, preferred_element_type=jnp.float32, precision=lax.Precision.HIGH)


def body(sigma_aa, l_as, block_mask):
    half_steps = lax.axis_size("row") // 2
    rows = sigma_aa.shape[0]
    sign = -block_mask[0, 0].astype(jnp.float32)
    cuts = [rows * cut // CUTS[-1] for cut in CUTS]
    pieces, block = [], sigma_aa
    for start, end in zip(cuts, cuts[1:]):
        piece, block = lax.optimization_barrier((block[start:end], block))
        pieces.append(piece)
    visits = [[shifted(piece, turn, -turn) for turn in range(1, half_steps)] for piece in pieces]
    first, second, third, last = [visit[-1] for visit in visits]

    def times_factor(block):
        return sign * product(block, l_as)

    def travel_back(total, piece):
        for visiting in reversed(visits[piece][:-1]):
            total = shifted(total, -1, 0) + times_factor(visiting)
        return shifted(total, -1, 0)

    first_total = times_factor(first)
    own = times_factor(after(sigma_aa, first_total))
    second_total = times_factor(after(second, own))
    first_out = travel_back(after(first_total, second_total, third), 0)
    second_out = travel_back(after(second_total, third), 1)
    third_total = times_factor(after(third, last, first_out))
    third_out = travel_back(third_total, 2)
    last_out = travel_back(times_factor(after(last, third_total)), 3)

    early = jnp.concatenate([first_out, second_out, third_out, jnp.zeros_like(last_out)], 0) + own
    return lax.dynamic_update_slice(early, last_out + own[cuts[3] :], (cuts[3], 0))


def solution(mesh):
    placed = (P(("fr", "row"), "col"), P(("fr", "row"), "col"), P(("fr", "row"), "col"))
    return jax.shard_map(
        body, mesh=mesh, in_specs=placed, out_specs=P(("fr", "row"), "col"), check_vma=False
    )
```

```python
import jax
import jax.numpy as jnp
from jax import lax
from jax.sharding import PartitionSpec as P


CUTS = (0, 3, 27, 46, 48)


def shifted(block, rows_by, cols_by):
    rows, cols = lax.axis_size("row"), lax.axis_size("col")
    route = [
        (r * cols + c, (r + rows_by) % rows * cols + (c + cols_by) % cols) for r in range(rows) for c in range(cols)
    ]
    return lax.ppermute(block, ("row", "col"), route)


def after(value, *others):
    return lax.optimization_barrier((value, *others))[0]


def product(lhs_block, rhs_block):
    return jnp.dot(lhs_block, rhs_block, preferred_element_type=jnp.float32, precision=lax.Precision.HIGH)


def body(sigma_aa, l_as, block_mask):
    half_steps = lax.axis_size("row") // 2
    rows = sigma_aa.shape[0]
    sign = -block_mask[0, 0].astype(jnp.float32)
    cuts = [rows * cut // CUTS[-1] for cut in CUTS]
    pieces, block = [], sigma_aa
    for start, end in zip(cuts, cuts[1:]):
        piece, block = lax.optimization_barrier((block[start:end], block))
        pieces.append(piece)
    visits = [[shifted(piece, turn, -turn) for turn in range(1, half_steps)] for piece in pieces]
    first, second, third, last = [visit[-1] for visit in visits]

    def times_factor(block):
        return sign * product(block, l_as)

    def travel_back(total, piece):
        for visiting in reversed(visits[piece][:-1]):
            total = shifted(total, -1, 0) + times_factor(visiting)
        return shifted(total, -1, 0)

    first_total = times_factor(first)
    own = times_factor(after(sigma_aa, first_total))
    second_total = times_factor(after(second, own))
    first_out = travel_back(after(first_total, second_total, third), 0)
    second_out = travel_back(after(second_total, third), 1)
    third_total = times_factor(after(third, last, first_out))
    third_out = travel_back(third_total, 2)
    last_out = travel_back(times_factor(after(last, third_total)), 3)

    early = jnp.concatenate([first_out, second_out, third_out, jnp.zeros_like(last_out)], 0) + own
    return lax.dynamic_update_slice(early, last_out + own[cuts[3] :], (cuts[3], 0))


def solution(mesh):
    placed = (P(("fr", "row"), "col"), P(("fr", "row"), "col"), P(("fr", "row"), "col"))
    return jax.shard_map(
        body, mesh=mesh, in_specs=placed, out_specs=P(("fr", "row"), "col"), check_vma=False
    )
```
